32 devices in a mesh: grp: 4 (over y, x), blk: 8 (over z, core).
Axes of the slice: x: 2, y: 2, z: 4, core: 2. Of those that a mesh axis runs over, the one named last changes fastest.
Arguments:
- queries: bfloat16 [4096, 4096], P(('grp', 'blk')), parts along dimension 0, may hold values from -256 to 256
- new_keys: bfloat16 [4096, 512], P(('grp', 'blk')), parts along dimension 0, may hold values from -6 to 6
- new_values: bfloat16 [4096, 512], P(('grp', 'blk')), parts along dimension 0, may hold values from -6 to 6
- prefix_keys: bfloat16 [4096, 512], P(('grp', 'blk')), parts along dimension 0, may hold values from -6 to 6
- prefix_values: bfloat16 [4096, 512], P(('grp', 'blk')), parts along dimension 0, may hold values from -6 to 6
- block_table: int32 [32, 8], P(('grp', 'blk')), parts along dimension 0, may hold values from 0 to 7, as said below
- prefix_blocks: int32 [32], P(('grp', 'blk')), parts along dimension 0, may hold values from 1 to 8, 40 in all
Outputs:
- attended: bfloat16 [4096, 4096], P(('grp', 'blk')), parts along dimension 0
The draws below stay inside these ranges and needn't reach their ends.
There are 4 independent parts, one for each index of `grp`. The reference program is written for one: setup_inputs(seed, part) draws one part's arguments, and reference() takes and returns one part's arrays. A program takes and returns all parts, laid end to end along the dimension named above; each array names one. Nothing has to cross between parts.
Inputs may be any that keep to these rules, and one draw needn't show every extreme that they name: `block_table`: each row names 8 different prefix blocks; only the first prefix_blocks entries of a row are read. `prefix_blocks`: within each group (each index of grp) the lengths sum to 40.
All inputs are finite; a program needn't handle non-finite values.
Results may differ from the reference program's by a relative error of at most 0.008.
Values may be sent and summed in bfloat16 or wider, within the bound.
A program may use at most 64 MiB of HBM per device.

```python
import math
import jax
import jax.numpy as jnp
import numpy as np
from jax import lax

H = 32
KVH = 4
DH = 128
BS = 128
NEW = 128
G = 8
REQUESTS = 8
POOL_BLOCKS = 8
MAXB = 8


def table_rows(key):
    row_keys = jax.random.split(jax.random.fold_in(key, 11), REQUESTS)
    return jax.vmap(lambda one: jax.random.permutation(one, POOL_BLOCKS)[:MAXB])(row_keys).astype(jnp.int32)


def key_field(key):
    base = jax.random.truncated_normal(jax.random.fold_in(key, 23), -6.0, 6.0, (POOL_BLOCKS, BS, KVH * DH), jnp.float32)
    return base


def draw_block_table(key, part):
    return table_rows(key)


def draw_prefix_keys(key, part):
    return key_field(key).reshape(POOL_BLOCKS * BS, KVH * DH).astype(jnp.bfloat16)


def draw_queries(key, part):
    base = jax.random.truncated_normal(jax.random.fold_in(key, 29), -6.0, 6.0, (REQUESTS, NEW, H * DH), jnp.float32)
    return base.reshape(REQUESTS * NEW, H * DH).astype(jnp.bfloat16)


def level_of(own_key, shape, pieces, low, high):
    def one(dim, parts):
        draws = jax.random.uniform(jax.random.fold_in(jax.random.fold_in(own_key, 6), dim), (parts,), jnp.float32, low / len(pieces), high / len(pieces))
        return jnp.repeat(jnp.exp(draws), shape[dim] // parts).reshape((-1,) + (1,) * (len(shape) - dim - 1))

    factor_of = one(*pieces[0])
    for cut in pieces[1:]:
        factor_of = factor_of * one(*cut)
    return factor_of


def length_profile(count, total, limit, lean):
    loads = [(1 << 20) // math.isqrt(standing ** lean) + 1 for standing in range(2, count + 1)]
    surplus, given = total - limit - (count - 1), [1] * (count - 1)
    while surplus > 0:
        candidates = [i for i in range(count - 1) if given[i] < limit]
        pool, remaining = sum([loads[i] for i in candidates]), surplus
        for i in candidates:
            addition = min(limit - given[i], max(1, remaining * loads[i] // pool), surplus)
            given[i] = given[i] + addition
            surplus = surplus - addition
    return np.array([limit] + given)


def ragged(key, count, total, reach, skew):
    if count == 2:
        one = jax.random.randint(key, (), max(1, total - reach), min(reach, total - 1) + 1)
        return jnp.stack([one, total - one])
    tallies = jnp.asarray(length_profile(count, total, reach, skew), jnp.int32)
    twos = (count - 1) // 2
    giver, receiver = tallies[1:1 + 2 * twos:2], tallies[2:2 + 2 * twos:2]
    slack = jnp.minimum(giver - 1, reach - receiver)
    passed = jax.random.randint(jax.random.fold_in(key, 1), (twos,), 0, 1 << 20) % (slack + 1)
    tallies = tallies.at[1:1 + 2 * twos:2].set(giver - passed).at[2:2 + 2 * twos:2].set(receiver + passed)
    return tallies[jax.random.permutation(jax.random.fold_in(key, 2), count)]


def normal_values(key, shape, scale, limit, cuts=(), held_as=jnp.bfloat16):
    loudness = level_of(key, shape, cuts, -0.22, 0.18) if cuts else 1.0
    values = jax.random.normal(key, shape, jnp.float32) * scale * loudness
    return jnp.minimum(jnp.maximum(values, -limit), limit).astype(held_as)


def setup_inputs(seed: int = 0, part: int = 0) -> dict:
    key_list = jax.random.split(jax.random.key(seed), 8)
    part_keys = jax.random.split(jax.random.fold_in(key_list[7], part), 8)
    queries = draw_queries(jax.random.fold_in(jax.random.fold_in(key_list[7], part), 71), part)
    new_keys = normal_values(part_keys[1], (REQUESTS * NEW, KVH * DH), 1.0, 6.0, ((0, 8),))
    new_values = normal_values(part_keys[2], (REQUESTS * NEW, KVH * DH), 1.0, 6.0, ((0, 8),))
    prefix_keys = draw_prefix_keys(jax.random.fold_in(jax.random.fold_in(key_list[7], part), 71), part)
    prefix_values = normal_values(part_keys[4], (POOL_BLOCKS * BS, KVH * DH), 1.0, 6.0, ((0, 8),))
    block_table = draw_block_table(jax.random.fold_in(jax.random.fold_in(key_list[7], part), 71), part)
    prefix_blocks = ragged(part_keys[6], REQUESTS, REQUESTS * MAXB * 5 // 8, MAXB, 1).astype(jnp.int32)
    return dict(queries=queries, new_keys=new_keys, new_values=new_values, prefix_keys=prefix_keys, prefix_values=prefix_values, block_table=block_table, prefix_blocks=prefix_blocks)


def reference(queries, new_keys, new_values, prefix_keys, prefix_values, block_table, prefix_blocks):
    scale = DH ** -0.5
    pool_keys = prefix_keys.reshape(POOL_BLOCKS, BS, KVH * DH)
    pool_values = prefix_values.reshape(POOL_BLOCKS, BS, KVH * DH)
    span = MAXB * BS + NEW
    position = jnp.arange(span, dtype=jnp.int32)
    token = jnp.arange(NEW, dtype=jnp.int32)

    def one_request(items):
        query, nkey, nvalue, row, length = items
        keys = jnp.concatenate([jnp.take(pool_keys, row, axis=0).reshape(MAXB * BS, KVH * DH), nkey], axis=0)
        values = jnp.concatenate([jnp.take(pool_values, row, axis=0).reshape(MAXB * BS, KVH * DH), nvalue], axis=0)
        qf = query.astype(jnp.float32).reshape(NEW, KVH, G, DH)
        kf = keys.astype(jnp.float32).reshape(span, KVH, DH)
        vf = values.astype(jnp.float32).reshape(span, KVH, DH)
        scores = jnp.einsum("nkgd,lkd->kgnl", qf, kf) * scale
        before = (position < MAXB * BS) & (position // BS < length)
        causal = (position[None, :] >= MAXB * BS) & (position[None, :] - MAXB * BS <= token[:, None])
        visible = before[None, :] | causal
        scores = jnp.where(visible[None, None], scores, -jnp.inf)
        top = jnp.max(scores, axis=-1, keepdims=True)
        weights = jnp.exp(scores - top)
        total = jnp.sum(weights, axis=-1)
        rounded = lax.optimization_barrier(weights.astype(jnp.bfloat16)).astype(jnp.float32)
        summed = jnp.einsum("kgnl,lkd->nkgd", rounded, vf)
        result = summed / jnp.transpose(total, (2, 0, 1))[..., None]
        return result.reshape(NEW, H * DH).astype(jnp.bfloat16)

    outputs = lax.map(one_request, (queries.reshape(REQUESTS, NEW, H * DH), new_keys.reshape(REQUESTS, NEW, KVH * DH), new_values.reshape(REQUESTS, NEW, KVH * DH), block_table.astype(jnp.int32), prefix_blocks.astype(jnp.int32)))
    return outputs.reshape(REQUESTS * NEW, H * DH)
```

```python
import functools

import jax
import jax.numpy as jnp
from jax import lax
from jax.experimental import pallas as pl
from jax.experimental.pallas import tpu as pltpu
from jax.sharding import PartitionSpec as P

DH = 128
BS = 128
MESH = pl.DeviceIdType.MESH
LOG2E = 1.4426950408889634
HIDDEN = 1e38
ROWS = 256


def kernel(
    chips, kvh, group, entries,
    table_ref, length_ref, q_hbm, nk_hbm, nv_hbm, pk_hbm, pv_hbm, out_hbm,
    qs, own, kv, acc, top, total, out, penalty,
    q_sem, own_sem, load_sem, out_sem, recv_line, recv_pair, send_line, send_right, send_pair,
):
    me = lax.axis_index("blk")
    chip = me // 2
    core = me - 2 * chip
    partner = 2 * chip + 1 - core
    rows = group * BS
    factor = LOG2E * DH ** -0.5
    has_left, has_right = chip > 0, chip < chips - 1

    barrier = pltpu.get_barrier_semaphore()

    def greet(device):
        pl.semaphore_signal(barrier, inc=1, device_id={"blk": device}, device_id_type=MESH)

    greet(partner)
    pl.when(has_left)(lambda: greet(me - 2))
    pl.when(has_right)(lambda: greet(me + 2))

    for h in range(kvh):
        cols = pl.ds(h * DH, DH)
        pltpu.make_async_copy(pk_hbm.at[:, cols], kv.at[chip, h, 0, core], load_sem.at[h]).start()
        pltpu.make_async_copy(pv_hbm.at[:, cols], kv.at[chip, h, 1, core], load_sem.at[h]).start()
    for h in range(kvh):
        cols = pl.ds(h * DH, DH)
        pltpu.make_async_copy(nk_hbm.at[:, cols], own.at[h, 0], own_sem.at[h]).start()
        pltpu.make_async_copy(nv_hbm.at[:, cols], own.at[h, 1], own_sem.at[h]).start()
        for g in range(group):
            pltpu.make_async_copy(
                q_hbm.at[:, pl.ds((h * group + g) * DH, DH)], qs.at[h, pl.ds(g * BS, BS)], q_sem.at[h]
            ).start()

    def line_copy(source, h, device, sem):
        piece = kv.at[source, h, :, core]
        return pltpu.make_async_remote_copy(
            src_ref=piece, dst_ref=piece, send_sem=sem, recv_sem=recv_line.at[source, h],
            device_id={"blk": device}, device_id_type=MESH,
        )

    def pair_copy(source, h):
        piece = kv.at[source, h, :, core]
        return pltpu.make_async_remote_copy(
            src_ref=piece, dst_ref=piece, send_sem=send_pair.at[source, h], recv_sem=recv_pair.at[source, h],
            device_id={"blk": partner}, device_id_type=MESH,
        )

    def to_left(source, h):
        return line_copy(source, h, me - 2, send_line.at[source, h])

    def to_right(source, h):
        return line_copy(source, h, me + 2, send_line.at[source, h])

    def own_right(h):
        return line_copy(chip, h, me + 2, send_right.at[h])

    pl.semaphore_wait(barrier, 1 + has_left.astype(jnp.int32) + has_right.astype(jnp.int32))
    for h in range(kvh):
        piece = kv.at[chip, h, :, core]
        pltpu.make_async_copy(piece, piece, load_sem.at[h]).wait()
        pl.when(has_left)(lambda: to_left(chip, h).start())
        pl.when(has_right)(lambda: own_right(h).start())
        pair_copy(chip, h).start()

    length = length_ref[0]
    for b in range(2 * chips):
        hits = [(table_ref[0, j] == b) & (j < length) for j in range(entries)]
        penalty[b] = jnp.where(functools.reduce(jnp.logical_or, hits), 0.0, HIDDEN)

    def scores_of(query, keys):
        return lax.dot_general(query, keys, (((1,), (1,)), ((), ())), preferred_element_type=jnp.float32)

    def own_tokens(h, _):
        pltpu.make_async_copy(qs.at[h], qs.at[h], q_sem.at[h]).wait()
        pltpu.make_async_copy(own.at[h], own.at[h], own_sem.at[h]).wait()
        keys, values = own[h, 0], own[h, 1]
        token = lax.broadcasted_iota(jnp.int32, (ROWS, BS), 0) % BS
        causal = lax.broadcasted_iota(jnp.int32, (ROWS, BS), 1) <= token
        for r in range(0, rows, ROWS):
            at = pl.ds(r, ROWS)
            scores = jnp.where(causal, scores_of(qs[h, at], keys), -HIDDEN)
            best = jnp.broadcast_to(jnp.max(scores, axis=-1, keepdims=True), (ROWS, DH))
            weights = jnp.exp2((scores - best) * factor)
            top[h, at] = best
            total[h, at] = weights
            acc[h, at] = jnp.dot(weights.astype(jnp.bfloat16), values, preferred_element_type=jnp.float32)
        return 0

    def absorb(source, h):
        keys = kv[source, h, 0].reshape(2 * BS, DH)
        values = kv[source, h, 1].reshape(2 * BS, DH)
        low, high = penalty[2 * source], penalty[2 * source + 1]
        for r in range(0, rows, ROWS):
            at = pl.ds(r, ROWS)
            scores = scores_of(qs[h, at], keys)
            first, second = scores[:, :BS] - low, scores[:, BS:] - high
            old = top[h, at]
            best = jnp.max(jnp.maximum(first, second), axis=-1, keepdims=True)
            best = jnp.maximum(old, jnp.broadcast_to(best, (ROWS, DH)))
            shrink = jnp.exp2((old - best) * factor)
            first = jnp.exp2((first - best) * factor)
            second = jnp.exp2((second - best) * factor)
            top[h, at] = best
            total[h, at] = shrink * total[h, at] + (first + second)
            weights = jnp.concatenate([first.astype(jnp.bfloat16), second.astype(jnp.bfloat16)], axis=1)
            acc[h, at] = shrink * acc[h, at] + jnp.dot(weights, values, preferred_element_type=jnp.float32)

    def out_copy(h):
        cols = pl.ds(pl.multiple_of(h * rows, DH), rows)
        return pltpu.make_async_copy(out.at[h], out_hbm.at[:, cols], out_sem.at[h])

    def finish(h):
        for g in range(group):
            at = pl.ds(g * BS, BS)
            whole = jnp.sum(total[h, at], axis=-1, keepdims=True)
            out[h, :, g * DH:(g + 1) * DH] = (acc[h, at] / whole).astype(jnp.bfloat16)
        out_copy(h).start()

    def own_chip(h, _):
        pair_copy(chip, h).wait_recv()
        absorb(chip, h)
        return 0

    def forward(i):
        far, h = 1 + i // kvh, i % kvh
        before, after = chip - far, chip + far

        @pl.when(after < chips)
        def _():
            line_copy(after, h, partner, send_line.at[after, h]).wait_recv()
            pl.when(has_left)(lambda: to_left(after, h).start())
            pair_copy(after, h).start()

        @pl.when(before >= 0)
        def _():
            line_copy(before, h, partner, send_line.at[before, h]).wait_recv()
            pl.when(has_right)(lambda: to_right(before, h).start())
            pair_copy(before, h).start()

    def sent(far, h):
        before, after = chip - far, chip + far

        @pl.when(after < chips)
        def _():
            pl.when(has_left)(lambda: to_left(after, h).wait_send())
            pair_copy(after, h).wait_send()

        @pl.when(before >= 0)
        def _():
            pl.when(has_right)(lambda: to_right(before, h).wait_send())
            pair_copy(before, h).wait_send()

    def own_sent(h):
        pl.when(has_left)(lambda: to_left(chip, h).wait_send())
        pl.when(has_right)(lambda: own_right(h).wait_send())
        pair_copy(chip, h).wait_send()

    def step(i, _):
        far, h = 1 + i // kvh, i % kvh
        before, after = chip - far, chip + far
        pl.when(i + 1 < kvh * (chips - 1))(lambda: forward(i + 1))
        pl.when(far == 1)(lambda: own_sent(h))
        pl.when(far > 1)(lambda: sent(far - 1, h))

        @pl.when(after < chips)
        def _():
            pair_copy(after, h).wait_recv()
            absorb(after, h)

        @pl.when(before >= 0)
        def _():
            pair_copy(before, h).wait_recv()
            absorb(before, h)

        pl.when(far == chips - 1)(lambda: finish(h))
        return 0

    lax.fori_loop(0, kvh, own_tokens, 0)
    lax.fori_loop(0, kvh, own_chip, 0)
    forward(0)
    lax.fori_loop(0, kvh * (chips - 1), step, 0)
    for h in range(kvh):
        sent(chips - 1, h)
        out_copy(h).wait()


def body(chips, queries, new_keys, new_values, prefix_keys, prefix_values, block_table, prefix_blocks):
    tokens, width = queries.shape
    kvh = new_keys.shape[1] // DH
    group = width // DH // kvh
    rows = group * tokens
    entries = block_table.shape[1]
    smem = pl.BlockSpec(memory_space=pltpu.SMEM)
    anywhere = pl.BlockSpec(memory_space=pl.ANY)
    dma = pltpu.SemaphoreType.DMA
    keys = (2 * chips + 1) * BS
    return pl.pallas_call(
        functools.partial(kernel, chips, kvh, group, entries),
        out_shape=jax.ShapeDtypeStruct((tokens, width), jnp.bfloat16),
        in_specs=[smem, smem] + [anywhere] * 5,
        out_specs=anywhere,
        scratch_shapes=[
            pltpu.VMEM((kvh, rows, DH), jnp.bfloat16),
            pltpu.VMEM((kvh, 2, tokens, DH), jnp.bfloat16),
            pltpu.VMEM((chips, kvh, 2, 2, BS, DH), jnp.bfloat16),
            pltpu.VMEM((kvh, rows, DH), jnp.float32),
            pltpu.VMEM((kvh, rows, DH), jnp.float32),
            pltpu.VMEM((kvh, rows, DH), jnp.float32),
            pltpu.VMEM((kvh, tokens, rows), jnp.bfloat16),
            pltpu.SMEM((2 * chips,), jnp.float32),
            dma((kvh,)),
            dma((kvh,)),
            dma((kvh,)),
            dma((kvh,)),
            dma((chips, kvh)),
            dma((chips, kvh)),
            dma((chips, kvh)),
            dma((kvh,)),
            dma((chips, kvh)),
        ],
        compiler_params=pltpu.CompilerParams(
            collective_id=0, has_side_effects=True, vmem_limit_bytes=48 * 1024 * 1024
        ),
        cost_estimate=pl.CostEstimate(
            flops=4 * kvh * rows * keys * DH, bytes_accessed=4 * tokens * width, transcendentals=kvh * rows * keys
        ),
    )(block_table, prefix_blocks, queries, new_keys, new_values, prefix_keys, prefix_values)


def solution(mesh):
    rows = P(("grp", "blk"), None)
    return jax.shard_map(
        functools.partial(body, mesh.shape["blk"] // 2),
        mesh=mesh,
        in_specs=(rows,) * 6 + (P(("grp", "blk")),),
        out_specs=rows,
        check_vma=False,
    )
```

```python
import functools

import jax
import jax.numpy as jnp
from jax import lax
from jax.experimental import pallas as pl
from jax.experimental.pallas import tpu as pltpu
from jax.sharding import PartitionSpec as P

DH = 128
BS = 128
MESH = pl.DeviceIdType.MESH
LOG2E = 1.4426950408889634
HIDDEN = 1e38
COLS = 256


def kernel(
    chips, kvh, group, entries,
    table_ref, length_ref, q_hbm, nk_hbm, nv_hbm, pk_hbm, pv_hbm, out_hbm,
    qs, qt, own, kv, acc, top, total, out, penalty,
    q_sem, own_sem, load_sem, out_sem, recv_line, recv_pair, send_line, send_right, send_pair,
):
    me = lax.axis_index("blk")
    chip = me // 2
    core = me - 2 * chip
    partner = 2 * chip + 1 - core
    rows = group * BS
    factor = LOG2E * DH ** -0.5
    has_left, has_right = chip > 0, chip < chips - 1

    barrier = pltpu.get_barrier_semaphore()

    def greet(device):
        pl.semaphore_signal(barrier, inc=1, device_id={"blk": device}, device_id_type=MESH)

    greet(partner)
    pl.when(has_left)(lambda: greet(me - 2))
    pl.when(has_right)(lambda: greet(me + 2))

    for h in range(kvh):
        cols = pl.ds(h * DH, DH)
        pltpu.make_async_copy(pk_hbm.at[:, cols], kv.at[chip, h, 0, core], load_sem.at[h]).start()
        pltpu.make_async_copy(pv_hbm.at[:, cols], kv.at[chip, h, 1, core], load_sem.at[h]).start()
    for h in range(kvh):
        cols = pl.ds(h * DH, DH)
        pltpu.make_async_copy(nk_hbm.at[:, cols], own.at[h, 0], own_sem.at[h]).start()
        pltpu.make_async_copy(nv_hbm.at[:, cols], own.at[h, 1], own_sem.at[h]).start()
        pltpu.make_async_copy(q_hbm.at[:, pl.ds(h * rows, rows)], qs.at[h], q_sem.at[h]).start()

    def line_copy(source, h, device, sem):
        piece = kv.at[source, h, :, core]
        return pltpu.make_async_remote_copy(
            src_ref=piece, dst_ref=piece, send_sem=sem, recv_sem=recv_line.at[source, h],
            device_id={"blk": device}, device_id_type=MESH,
        )

    def pair_copy(source, h):
        piece = kv.at[source, h, :, core]
        return pltpu.make_async_remote_copy(
            src_ref=piece, dst_ref=piece, send_sem=send_pair.at[source, h], recv_sem=recv_pair.at[source, h],
            device_id={"blk": partner}, device_id_type=MESH,
        )

    def to_left(source, h):
        return line_copy(source, h, me - 2, send_line.at[source, h])

    def to_right(source, h):
        return line_copy(source, h, me + 2, send_line.at[source, h])

    def own_right(h):
        return line_copy(chip, h, me + 2, send_right.at[h])

    pl.semaphore_wait(barrier, 1 + has_left.astype(jnp.int32) + has_right.astype(jnp.int32))
    for h in range(kvh):
        piece = kv.at[chip, h, :, core]
        pltpu.make_async_copy(piece, piece, load_sem.at[h]).wait()
        pl.when(has_left)(lambda: to_left(chip, h).start())
        pl.when(has_right)(lambda: own_right(h).start())
        pair_copy(chip, h).start()

    length = length_ref[0]
    for b in range(2 * chips):
        hits = [(table_ref[0, j] == b) & (j < length) for j in range(entries)]
        penalty[b] = jnp.where(functools.reduce(jnp.logical_or, hits), 0.0, HIDDEN)

    def own_tokens(h, _):
        pltpu.make_async_copy(qs.at[h], qs.at[h], q_sem.at[h]).wait()
        pltpu.make_async_copy(own.at[h], own.at[h], own_sem.at[h]).wait()
        for g in range(group):
            at = pl.ds(g * BS, BS)
            qt[h, :, at] = jnp.transpose(qs[h, :, at])
        keys, values = own[h, 0], jnp.transpose(own[h, 1])
        token = lax.broadcasted_iota(jnp.int32, (BS, COLS), 1) % BS
        causal = lax.broadcasted_iota(jnp.int32, (BS, COLS), 0) <= token
        for c in range(0, rows, COLS):
            at = pl.ds(c, COLS)
            scores = jnp.dot(keys, qt[h, :, at], preferred_element_type=jnp.float32)
            scores = jnp.where(causal, scores, -HIDDEN).reshape(BS // 8, 8, COLS)
            best = jnp.max(jnp.max(scores, axis=0), axis=0, keepdims=True)
            best = jnp.broadcast_to(best, (8, COLS))
            weights = jnp.exp2((scores - best[None]) * factor)
            top[h, :, at] = best
            total[h, :, at] = jnp.sum(weights, axis=0)
            weights = weights.reshape(BS, COLS).astype(jnp.bfloat16)
            acc[h, :, at] = jnp.dot(values, weights, preferred_element_type=jnp.float32)
        return 0

    def absorb(source, h):
        keys = kv[source, h, 0].reshape(2 * BS, DH)
        values = jnp.transpose(kv[source, h, 1].reshape(2 * BS, DH))
        low, high = penalty[2 * source], penalty[2 * source + 1]
        for c in range(0, rows, COLS):
            at = pl.ds(c, COLS)
            scores = jnp.dot(keys, qt[h, :, at], preferred_element_type=jnp.float32)
            scores = scores.reshape(2, BS // 8, 8, COLS)
            peak = jnp.max(scores, axis=1)
            best = jnp.max(jnp.maximum(peak[0] - low, peak[1] - high), axis=0, keepdims=True)
            old = top[h, :, at]
            best = jnp.maximum(old, jnp.broadcast_to(best, (8, COLS)))
            shrink = jnp.exp2((old - best) * factor)
            first = jnp.exp2((scores[0] - (best + low)[None]) * factor)
            second = jnp.exp2((scores[1] - (best + high)[None]) * factor)
            top[h, :, at] = best
            total[h, :, at] = shrink * total[h, :, at] + (jnp.sum(first, axis=0) + jnp.sum(second, axis=0))
            weights = jnp.concatenate(
                [first.reshape(BS, COLS).astype(jnp.bfloat16), second.reshape(BS, COLS).astype(jnp.bfloat16)], axis=0
            )
            kept = (acc[h, :, at].reshape(DH // 8, 8, COLS) * shrink[None]).reshape(DH, COLS)
            acc[h, :, at] = kept + jnp.dot(values, weights, preferred_element_type=jnp.float32)

    def out_copy(h):
        cols = pl.ds(pl.multiple_of(h * rows, DH), rows)
        return pltpu.make_async_copy(out.at[h], out_hbm.at[:, cols], out_sem.at[h])

    def finish(h):
        for g in range(group):
            at = pl.ds(g * BS, BS)
            share = 1.0 / jnp.sum(total[h, :, at], axis=0, keepdims=True)
            out[h, :, at] = jnp.transpose(acc[h, :, at] * share).astype(jnp.bfloat16)
        out_copy(h).start()

    def own_chip(h, _):
        pair_copy(chip, h).wait_recv()
        absorb(chip, h)
        return 0

    def forward(i):
        far, h = 1 + i // kvh, i % kvh
        before, after = chip - far, chip + far

        @pl.when(after < chips)
        def _():
            line_copy(after, h, partner, send_line.at[after, h]).wait_recv()
            pl.when(has_left)(lambda: to_left(after, h).start())
            pair_copy(after, h).start()

        @pl.when(before >= 0)
        def _():
            line_copy(before, h, partner, send_line.at[before, h]).wait_recv()
            pl.when(has_right)(lambda: to_right(before, h).start())
            pair_copy(before, h).start()

    def sent(far, h):
        before, after = chip - far, chip + far

        @pl.when(after < chips)
        def _():
            pl.when(has_left)(lambda: to_left(after, h).wait_send())
            pair_copy(after, h).wait_send()

        @pl.when(before >= 0)
        def _():
            pl.when(has_right)(lambda: to_right(before, h).wait_send())
            pair_copy(before, h).wait_send()

    def own_sent(h):
        pl.when(has_left)(lambda: to_left(chip, h).wait_send())
        pl.when(has_right)(lambda: own_right(h).wait_send())
        pair_copy(chip, h).wait_send()

    def step(i, _):
        far, h = 1 + i // kvh, i % kvh
        before, after = chip - far, chip + far
        pl.when(i + 1 < kvh * (chips - 1))(lambda: forward(i + 1))
        pl.when(far == 1)(lambda: own_sent(h))
        pl.when(far > 1)(lambda: sent(far - 1, h))

        @pl.when(after < chips)
        def _():
            pair_copy(after, h).wait_recv()
            absorb(after, h)

        @pl.when(before >= 0)
        def _():
            pair_copy(before, h).wait_recv()
            absorb(before, h)

        pl.when(far == chips - 1)(lambda: finish(h))
        return 0

    lax.fori_loop(0, kvh, own_tokens, 0)
    lax.fori_loop(0, kvh, own_chip, 0)
    forward(0)
    lax.fori_loop(0, kvh * (chips - 1), step, 0)
    for h in range(kvh):
        sent(chips - 1, h)
        out_copy(h).wait()


def body(chips, queries, new_keys, new_values, prefix_keys, prefix_values, block_table, prefix_blocks):
    tokens, width = queries.shape
    kvh = new_keys.shape[1] // DH
    group = width // DH // kvh
    rows = group * tokens
    entries = block_table.shape[1]
    smem = pl.BlockSpec(memory_space=pltpu.SMEM)
    hbm = pl.BlockSpec(memory_space=pltpu.HBM)
    dma = pltpu.SemaphoreType.DMA
    keys = (2 * chips + 1) * BS
    return pl.pallas_call(
        functools.partial(kernel, chips, kvh, group, entries),
        out_shape=jax.ShapeDtypeStruct((tokens, width), jnp.bfloat16),
        in_specs=[smem, smem] + [hbm] * 5,
        out_specs=hbm,
        scratch_shapes=[
            pltpu.VMEM((kvh, tokens, rows), jnp.bfloat16),
            pltpu.VMEM((kvh, DH, rows), jnp.bfloat16),
            pltpu.VMEM((kvh, 2, tokens, DH), jnp.bfloat16),
            pltpu.VMEM((chips, kvh, 2, 2, BS, DH), jnp.bfloat16),
            pltpu.VMEM((kvh, DH, rows), jnp.float32),
            pltpu.VMEM((kvh, 8, rows), jnp.float32),
            pltpu.VMEM((kvh, 8, rows), jnp.float32),
            pltpu.VMEM((kvh, tokens, rows), jnp.bfloat16),
            pltpu.SMEM((2 * chips,), jnp.float32),
            dma((kvh,)),
            dma((kvh,)),
            dma((kvh,)),
            dma((kvh,)),
            dma((chips, kvh)),
            dma((chips, kvh)),
            dma((chips, kvh)),
            dma((kvh,)),
            dma((chips, kvh)),
        ],
        compiler_params=pltpu.CompilerParams(
            collective_id=0, has_side_effects=True, vmem_limit_bytes=60 * 1024 * 1024
        ),
        cost_estimate=pl.CostEstimate(
            flops=4 * kvh * rows * keys * DH, bytes_accessed=4 * tokens * width, transcendentals=kvh * rows * keys
        ),
    )(block_table, prefix_blocks, queries, new_keys, new_values, prefix_keys, prefix_values)


def solution(mesh):
    rows = P(("grp", "blk"), None)
    return jax.shard_map(
        functools.partial(body, mesh.shape["blk"] // 2),
        mesh=mesh,
        in_specs=(rows,) * 6 + (P(("grp", "blk")),),
        out_specs=rows,
        check_vma=False,
    )
```

```python
import functools

import jax
import jax.numpy as jnp
from jax import lax
from jax.experimental import pallas as pl
from jax.experimental.pallas import tpu as pltpu
from jax.sharding import PartitionSpec as P

DH = 128
BS = 128
MESH = pl.DeviceIdType.MESH
LOG2E = 1.4426950408889634
HIDDEN = 1e38


def kernel(
    chips, kvh, group, entries,
    table_ref, length_ref, q_hbm, nk_hbm, nv_hbm, pk_hbm, pv_hbm, out_hbm,
    qs, own, kv, acc, top, total, out, penalty,
    q_sem, own_sem, load_sem, out_sem, recv_line, recv_pair, send_line, send_right, send_pair,
):
    me = lax.axis_index("blk")
    chip = me // 2
    core = me - 2 * chip
    partner = 2 * chip + 1 - core
    rows = group * BS
    factor = LOG2E * DH ** -0.5
    has_left, has_right = chip > 0, chip < chips - 1

    barrier = pltpu.get_barrier_semaphore()

    def greet(device):
        pl.semaphore_signal(barrier, inc=1, device_id={"blk": device}, device_id_type=MESH)

    greet(partner)
    pl.when(has_left)(lambda: greet(me - 2))
    pl.when(has_right)(lambda: greet(me + 2))

    for h in range(kvh):
        cols = pl.ds(h * DH, DH)
        pltpu.make_async_copy(pk_hbm.at[:, cols], kv.at[chip, h, 0, core], load_sem.at[h]).start()
        pltpu.make_async_copy(pv_hbm.at[:, cols], kv.at[chip, h, 1, core], load_sem.at[h]).start()
    for h in range(kvh):
        cols = pl.ds(h * DH, DH)
        pltpu.make_async_copy(nk_hbm.at[:, cols], own.at[h, 0], own_sem.at[h]).start()
        pltpu.make_async_copy(nv_hbm.at[:, cols], own.at[h, 1], own_sem.at[h]).start()
        for g in range(group):
            pltpu.make_async_copy(
                q_hbm.at[:, pl.ds((h * group + g) * DH, DH)], qs.at[h, pl.ds(g * BS, BS)], q_sem.at[h]
            ).start()

    def line_copy(source, h, device, sem):
        piece = kv.at[source, h, :, core]
        return pltpu.make_async_remote_copy(
            src_ref=piece, dst_ref=piece, send_sem=sem, recv_sem=recv_line.at[source, h],
            device_id={"blk": device}, device_id_type=MESH,
        )

    def pair_copy(source, h):
        piece = kv.at[source, h, :, core]
        return pltpu.make_async_remote_copy(
            src_ref=piece, dst_ref=piece, send_sem=send_pair.at[source, h], recv_sem=recv_pair.at[source, h],
            device_id={"blk": partner}, device_id_type=MESH,
        )

    def to_left(source, h):
        return line_copy(source, h, me - 2, send_line.at[source, h])

    def to_right(source, h):
        return line_copy(source, h, me + 2, send_line.at[source, h])

    def own_right(h):
        return line_copy(chip, h, me + 2, send_right.at[h])

    pl.semaphore_wait(barrier, 1 + has_left.astype(jnp.int32) + has_right.astype(jnp.int32))
    for h in range(kvh):
        piece = kv.at[chip, h, :, core]
        pltpu.make_async_copy(piece, piece, load_sem.at[h]).wait()
        pl.when(has_left)(lambda: to_left(chip, h).start())
        pl.when(has_right)(lambda: own_right(h).start())
        pair_copy(chip, h).start()

    length = length_ref[0]
    for b in range(2 * chips):
        hits = [(table_ref[0, j] == b) & (j < length) for j in range(entries)]
        penalty[b] = jnp.where(functools.reduce(jnp.logical_or, hits), 0.0, HIDDEN)

    def scores_of(query, keys):
        return lax.dot_general(query, keys, (((1,), (1,)), ((), ())), preferred_element_type=jnp.float32)

    def own_tokens(h, _):
        pltpu.make_async_copy(qs.at[h], qs.at[h], q_sem.at[h]).wait()
        pltpu.make_async_copy(own.at[h], own.at[h], own_sem.at[h]).wait()
        token = lax.broadcasted_iota(jnp.int32, (rows, BS), 0) % BS
        causal = lax.broadcasted_iota(jnp.int32, (rows, BS), 1) <= token
        scores = jnp.where(causal, scores_of(qs[h], own[h, 0]), -HIDDEN)
        best = jnp.broadcast_to(jnp.max(scores, axis=-1, keepdims=True), (rows, DH))
        weights = jnp.exp2((scores - best) * factor)
        summed = jnp.dot(weights.astype(jnp.bfloat16), own[h, 1], preferred_element_type=jnp.float32)
        top[h] = best
        total[h] = weights
        acc[h] = summed
        return 0

    def absorb(source, h):
        keys = kv[source, h, 0].reshape(2 * BS, DH)
        values = kv[source, h, 1].reshape(2 * BS, DH)
        low, high = penalty[2 * source], penalty[2 * source + 1]
        old, old_total, old_acc = top[h], total[h], acc[h]
        scores = scores_of(qs[h], keys)
        first, second = scores[:, :BS] - low, scores[:, BS:] - high
        best = jnp.max(jnp.maximum(first, second), axis=-1, keepdims=True)
        best = jnp.maximum(old, jnp.broadcast_to(best, (rows, DH)))
        shrink = jnp.exp2((old - best) * factor)
        first = jnp.exp2((first - best) * factor)
        second = jnp.exp2((second - best) * factor)
        weights = jnp.concatenate([first.astype(jnp.bfloat16), second.astype(jnp.bfloat16)], axis=1)
        summed = jnp.dot(weights, values, preferred_element_type=jnp.float32)
        top[h] = best
        total[h] = shrink * old_total + (first + second)
        acc[h] = shrink * old_acc + summed

    def out_copy(h):
        cols = pl.ds(pl.multiple_of(h * rows, DH), rows)
        return pltpu.make_async_copy(out.at[h], out_hbm.at[:, cols], out_sem.at[h])

    def finish(h):
        for g in range(group):
            at = pl.ds(g * BS, BS)
            whole = jnp.sum(total[h, at], axis=-1, keepdims=True)
            out[h, :, g * DH:(g + 1) * DH] = (acc[h, at] / whole).astype(jnp.bfloat16)
        out_copy(h).start()

    def own_chip(h, _):
        pair_copy(chip, h).wait_recv()
        absorb(chip, h)
        return 0

    def forward(i):
        far, h = 1 + i // kvh, i % kvh
        before, after = chip - far, chip + far

        @pl.when(after < chips)
        def _():
            line_copy(after, h, partner, send_line.at[after, h]).wait_recv()
            pl.when(has_left)(lambda: to_left(after, h).start())
            pair_copy(after, h).start()

        @pl.when(before >= 0)
        def _():
            line_copy(before, h, partner, send_line.at[before, h]).wait_recv()
            pl.when(has_right)(lambda: to_right(before, h).start())
            pair_copy(before, h).start()

    def sent(far, h):
        before, after = chip - far, chip + far

        @pl.when(after < chips)
        def _():
            pl.when(has_left)(lambda: to_left(after, h).wait_send())
            pair_copy(after, h).wait_send()

        @pl.when(before >= 0)
        def _():
            pl.when(has_right)(lambda: to_right(before, h).wait_send())
            pair_copy(before, h).wait_send()

    def own_sent(h):
        pl.when(has_left)(lambda: to_left(chip, h).wait_send())
        pl.when(has_right)(lambda: own_right(h).wait_send())
        pair_copy(chip, h).wait_send()

    def step(i, _):
        far, h = 1 + i // kvh, i % kvh
        before, after = chip - far, chip + far
        pl.when(i + 1 < kvh * (chips - 1))(lambda: forward(i + 1))
        pl.when(far == 1)(lambda: own_sent(h))
        pl.when(far > 1)(lambda: sent(far - 1, h))

        @pl.when(after < chips)
        def _():
            pair_copy(after, h).wait_recv()
            absorb(after, h)

        @pl.when(before >= 0)
        def _():
            pair_copy(before, h).wait_recv()
            absorb(before, h)

        pl.when(far == chips - 1)(lambda: finish(h))
        return 0

    lax.fori_loop(0, kvh, own_tokens, 0)
    lax.fori_loop(0, kvh, own_chip, 0)
    forward(0)
    lax.fori_loop(0, kvh * (chips - 1), step, 0)
    for h in range(kvh):
        sent(chips - 1, h)
        out_copy(h).wait()


def body(chips, queries, new_keys, new_values, prefix_keys, prefix_values, block_table, prefix_blocks):
    tokens, width = queries.shape
    kvh = new_keys.shape[1] // DH
    group = width // DH // kvh
    rows = group * tokens
    entries = block_table.shape[1]
    smem = pl.BlockSpec(memory_space=pltpu.SMEM)
    anywhere = pl.BlockSpec(memory_space=pl.ANY)
    dma = pltpu.SemaphoreType.DMA
    keys = (2 * chips + 1) * BS
    return pl.pallas_call(
        functools.partial(kernel, chips, kvh, group, entries),
        out_shape=jax.ShapeDtypeStruct((tokens, width), jnp.bfloat16),
        in_specs=[smem, smem] + [anywhere] * 5,
        out_specs=anywhere,
        scratch_shapes=[
            pltpu.VMEM((kvh, rows, DH), jnp.bfloat16),
            pltpu.VMEM((kvh, 2, tokens, DH), jnp.bfloat16),
            pltpu.VMEM((chips, kvh, 2, 2, BS, DH), jnp.bfloat16),
            pltpu.VMEM((kvh, rows, DH), jnp.float32),
            pltpu.VMEM((kvh, rows, DH), jnp.float32),
            pltpu.VMEM((kvh, rows, DH), jnp.float32),
            pltpu.VMEM((kvh, tokens, rows), jnp.bfloat16),
            pltpu.SMEM((2 * chips,), jnp.float32),
            dma((kvh,)),
            dma((kvh,)),
            dma((kvh,)),
            dma((kvh,)),
            dma((chips, kvh)),
            dma((chips, kvh)),
            dma((chips, kvh)),
            dma((kvh,)),
            dma((chips, kvh)),
        ],
        compiler_params=pltpu.CompilerParams(
            collective_id=0, has_side_effects=True, vmem_limit_bytes=60 * 1024 * 1024
        ),
        cost_estimate=pl.CostEstimate(
            flops=4 * kvh * rows * keys * DH, bytes_accessed=4 * tokens * width, transcendentals=kvh * rows * keys
        ),
    )(block_table, prefix_blocks, queries, new_keys, new_values, prefix_keys, prefix_values)


def solution(mesh):
    rows = P(("grp", "blk"), None)
    return jax.shard_map(
        functools.partial(body, mesh.shape["blk"] // 2),
        mesh=mesh,
        in_specs=(rows,) * 6 + (P(("grp", "blk")),),
        out_specs=rows,
        check_vma=False,
    )
```

```python
import functools

import jax
import jax.numpy as jnp
from jax import lax
from jax.experimental import pallas as pl
from jax.experimental.pallas import tpu as pltpu
from jax.sharding import PartitionSpec as P

DH = 128
BS = 128
MESH = pl.DeviceIdType.MESH
LOG2E = 1.4426950408889634
HIDDEN = 1e38


def kernel(
    chips, kvh, group, entries,
    table_ref, length_ref, q_hbm, nk_hbm, nv_hbm, pk_hbm, pv_hbm, out,
    qs, own, kv, acc, top, total, penalty,
    q_sem, own_sem, load_sem, recv_line, recv_pair, send_line, send_right, send_pair,
):
    me = lax.axis_index("blk")
    chip = me // 2
    core = me - 2 * chip
    partner = 2 * chip + 1 - core
    rows = group * BS
    factor = LOG2E * DH ** -0.5
    has_left, has_right = chip > 0, chip < chips - 1

    barrier = pltpu.get_barrier_semaphore()

    def greet(device):
        pl.semaphore_signal(barrier, inc=1, device_id={"blk": device}, device_id_type=MESH)

    greet(partner)
    pl.when(has_left)(lambda: greet(me - 2))
    pl.when(has_right)(lambda: greet(me + 2))

    for h in range(kvh):
        cols = pl.ds(h * DH, DH)
        pltpu.make_async_copy(pk_hbm.at[:, cols], kv.at[chip, h, 0, core], load_sem.at[h]).start()
        pltpu.make_async_copy(pv_hbm.at[:, cols], kv.at[chip, h, 1, core], load_sem.at[h]).start()
    def line_copy(source, h, device, sem):
        piece = kv.at[source, h, :, core]
        return pltpu.make_async_remote_copy(
            src_ref=piece, dst_ref=piece, send_sem=sem, recv_sem=recv_line.at[source, h],
            device_id={"blk": device}, device_id_type=MESH,
        )

    def pair_copy(source, h):
        piece = kv.at[source, h, :, core]
        return pltpu.make_async_remote_copy(
            src_ref=piece, dst_ref=piece, send_sem=send_pair.at[source, h], recv_sem=recv_pair.at[source, h],
            device_id={"blk": partner}, device_id_type=MESH,
        )

    def to_left(source, h):
        return line_copy(source, h, me - 2, send_line.at[source, h])

    def to_right(source, h):
        return line_copy(source, h, me + 2, send_line.at[source, h])

    def own_right(h):
        return line_copy(chip, h, me + 2, send_right.at[h])

    pl.semaphore_wait(barrier, 1 + has_left.astype(jnp.int32) + has_right.astype(jnp.int32))
    for h in range(kvh):
        piece = kv.at[chip, h, :, core]
        pltpu.make_async_copy(piece, piece, load_sem.at[h]).wait()
        pl.when(has_left)(lambda: to_left(chip, h).start())
        pl.when(has_right)(lambda: own_right(h).start())
        pair_copy(chip, h).start()

    for h in range(kvh):
        cols = pl.ds(h * DH, DH)
        pltpu.make_async_copy(nk_hbm.at[:, cols], own.at[h, 0], own_sem.at[h]).start()
        pltpu.make_async_copy(nv_hbm.at[:, cols], own.at[h, 1], own_sem.at[h]).start()
        for g in range(group):
            pltpu.make_async_copy(
                q_hbm.at[:, pl.ds((h * group + g) * DH, DH)], qs.at[h, pl.ds(g * BS, BS)], q_sem.at[h]
            ).start()

    length = length_ref[0]
    for b in range(2 * chips):
        hits = [(table_ref[0, j] == b) & (j < length) for j in range(entries)]
        penalty[b] = jnp.where(functools.reduce(jnp.logical_or, hits), 0.0, HIDDEN)

    def scores_of(query, keys):
        return lax.dot_general(query, keys, (((1,), (1,)), ((), ())), preferred_element_type=jnp.float32)

    def own_tokens(h, _):
        pltpu.make_async_copy(qs.at[h], qs.at[h], q_sem.at[h]).wait()
        pltpu.make_async_copy(own.at[h], own.at[h], own_sem.at[h]).wait()
        token = lax.broadcasted_iota(jnp.int32, (rows, BS), 0) % BS
        causal = lax.broadcasted_iota(jnp.int32, (rows, BS), 1) <= token
        scores = jnp.where(causal, scores_of(qs[h], own[h, 0]), -HIDDEN)
        best = jnp.broadcast_to(jnp.max(scores, axis=-1, keepdims=True), (rows, DH))
        weights = jnp.exp2((scores - best) * factor)
        summed = jnp.dot(weights.astype(jnp.bfloat16), own[h, 1], preferred_element_type=jnp.float32)
        top[h] = best
        total[h] = weights
        acc[h] = summed
        return 0

    def absorb(source, h):
        keys = kv[source, h, 0].reshape(2 * BS, DH)
        values = kv[source, h, 1].reshape(2 * BS, DH)
        low, high = penalty[2 * source], penalty[2 * source + 1]
        old, old_total, old_acc = top[h], total[h], acc[h]
        scores = scores_of(qs[h], keys)
        first, second = scores[:, :BS] - low, scores[:, BS:] - high
        best = jnp.max(jnp.maximum(first, second), axis=-1, keepdims=True)
        best = jnp.maximum(old, jnp.broadcast_to(best, (rows, DH)))
        shrink = jnp.exp2((old - best) * factor)
        first = jnp.exp2((first - best) * factor)
        second = jnp.exp2((second - best) * factor)
        weights = jnp.concatenate([first.astype(jnp.bfloat16), second.astype(jnp.bfloat16)], axis=1)
        summed = jnp.dot(weights, values, preferred_element_type=jnp.float32)
        top[h] = best
        total[h] = shrink * old_total + (first + second)
        acc[h] = shrink * old_acc + summed

    def finish(h):
        whole = jnp.sum(total[h], axis=-1, keepdims=True)
        result = (acc[h] * (1.0 / whole)).astype(jnp.bfloat16)
        for g in range(group):
            cols = pl.ds(pl.multiple_of((h * group + g) * DH, DH), DH)
            out[:, cols] = result[g * BS:(g + 1) * BS]

    def own_chip(h, _):
        pair_copy(chip, h).wait_recv()
        absorb(chip, h)
        return 0

    def forward(i):
        far, h = 1 + i // kvh, i % kvh
        before, after = chip - far, chip + far

        @pl.when(after < chips)
        def _():
            line_copy(after, h, partner, send_line.at[after, h]).wait_recv()
            pl.when(has_left)(lambda: to_left(after, h).start())
            pair_copy(after, h).start()

        @pl.when(before >= 0)
        def _():
            line_copy(before, h, partner, send_line.at[before, h]).wait_recv()
            pl.when(has_right)(lambda: to_right(before, h).start())
            pair_copy(before, h).start()

    def sent(far, h):
        before, after = chip - far, chip + far

        @pl.when(after < chips)
        def _():
            pl.when(has_left)(lambda: to_left(after, h).wait_send())
            pair_copy(after, h).wait_send()

        @pl.when(before >= 0)
        def _():
            pl.when(has_right)(lambda: to_right(before, h).wait_send())
            pair_copy(before, h).wait_send()

    def own_sent(h):
        pl.when(has_left)(lambda: to_left(chip, h).wait_send())
        pl.when(has_right)(lambda: own_right(h).wait_send())
        pair_copy(chip, h).wait_send()

    def step(i, _):
        far, h = 1 + i // kvh, i % kvh
        before, after = chip - far, chip + far
        pl.when(i + 1 < kvh * (chips - 1))(lambda: forward(i + 1))
        pl.when(far == 1)(lambda: own_sent(h))
        pl.when(far > 1)(lambda: sent(far - 1, h))

        @pl.when(after < chips)
        def _():
            pair_copy(after, h).wait_recv()
            absorb(after, h)

        @pl.when(before >= 0)
        def _():
            pair_copy(before, h).wait_recv()
            absorb(before, h)

        pl.when(far == chips - 1)(lambda: finish(h))
        return 0

    lax.fori_loop(0, kvh, own_tokens, 0)
    lax.fori_loop(0, kvh, own_chip, 0)
    forward(0)
    lax.fori_loop(0, kvh * (chips - 1), step, 0)
    for h in range(kvh):
        sent(chips - 1, h)


def body(chips, queries, new_keys, new_values, prefix_keys, prefix_values, block_table, prefix_blocks):
    tokens, width = queries.shape
    kvh = new_keys.shape[1] // DH
    group = width // DH // kvh
    rows = group * tokens
    entries = block_table.shape[1]
    smem = pl.BlockSpec(memory_space=pltpu.SMEM)
    anywhere = pl.BlockSpec(memory_space=pl.ANY)
    dma = pltpu.SemaphoreType.DMA
    keys = (2 * chips + 1) * BS
    return pl.pallas_call(
        functools.partial(kernel, chips, kvh, group, entries),
        out_shape=pltpu.VMEM((tokens, width), jnp.bfloat16),
        in_specs=[smem, smem] + [anywhere] * 5,
        out_specs=pl.BlockSpec(memory_space=pltpu.VMEM),
        scratch_shapes=[
            pltpu.VMEM((kvh, rows, DH), jnp.bfloat16),
            pltpu.VMEM((kvh, 2, tokens, DH), jnp.bfloat16),
            pltpu.VMEM((chips, kvh, 2, 2, BS, DH), jnp.bfloat16),
            pltpu.VMEM((kvh, rows, DH), jnp.float32),
            pltpu.VMEM((kvh, rows, DH), jnp.float32),
            pltpu.VMEM((kvh, rows, DH), jnp.float32),
            pltpu.SMEM((2 * chips,), jnp.float32),
            dma((kvh,)),
            dma((kvh,)),
            dma((kvh,)),
            dma((chips, kvh)),
            dma((chips, kvh)),
            dma((chips, kvh)),
            dma((kvh,)),
            dma((chips, kvh)),
        ],
        compiler_params=pltpu.CompilerParams(
            collective_id=0, has_side_effects=True, vmem_limit_bytes=57 * 1024 * 1024
        ),
        cost_estimate=pl.CostEstimate(
            flops=4 * kvh * rows * keys * DH, bytes_accessed=4 * tokens * width, transcendentals=kvh * rows * keys
        ),
    )(block_table, prefix_blocks, queries, new_keys, new_values, prefix_keys, prefix_values)


def solution(mesh):
    rows = P(("grp", "blk"), None)
    return jax.shard_map(
        functools.partial(body, mesh.shape["blk"] // 2),
        mesh=mesh,
        in_specs=(rows,) * 6 + (P(("grp", "blk")),),
        out_specs=rows,
        check_vma=False,
    )
```

```python
import functools

import jax
import jax.numpy as jnp
from jax import lax
from jax.experimental import pallas as pl
from jax.experimental.pallas import tpu as pltpu
from jax.sharding import PartitionSpec as P

DH = 128
BS = 128
MESH = pl.DeviceIdType.MESH
LOG2E = 1.4426950408889634
HIDDEN = 1e38


def kernel(
    chips, kvh, group, entries,
    table_ref, length_ref, q_hbm, nk_hbm, nv_hbm, pk_hbm, pv_hbm, out,
    qs, own, kv, acc, top, total, penalty,
    q_sem, own_sem, load_sem, recv_line, recv_pair, send_line, send_right, send_pair,
):
    me = lax.axis_index("blk")
    chip = me // 2
    core = me - 2 * chip
    partner = 2 * chip + 1 - core
    rows = group * BS
    factor = LOG2E * DH ** -0.5
    has_left, has_right = chip > 0, chip < chips - 1
    inner = has_left & has_right
    items = kvh * (chips - 1)

    barrier = pltpu.get_barrier_semaphore()

    def greet(device):
        pl.semaphore_signal(barrier, inc=1, device_id={"blk": device}, device_id_type=MESH)

    greet(partner)
    pl.when(has_left)(lambda: greet(me - 2))
    pl.when(has_right)(lambda: greet(me + 2))

    for h in range(kvh):
        cols = pl.ds(h * DH, DH)
        pltpu.make_async_copy(pk_hbm.at[:, cols], kv.at[chip, h, 0, core], load_sem.at[h]).start()
        pltpu.make_async_copy(pv_hbm.at[:, cols], kv.at[chip, h, 1, core], load_sem.at[h]).start()
    def line_copy(source, h, device, sem):
        piece = kv.at[source, h, :, core]
        return pltpu.make_async_remote_copy(
            src_ref=piece, dst_ref=piece, send_sem=sem, recv_sem=recv_line.at[source, h],
            device_id={"blk": device}, device_id_type=MESH,
        )

    def pair_copy(source, h):
        piece = kv.at[source, h, :, core]
        return pltpu.make_async_remote_copy(
            src_ref=piece, dst_ref=piece, send_sem=send_pair.at[source, h], recv_sem=recv_pair.at[source, h],
            device_id={"blk": partner}, device_id_type=MESH,
        )

    def to_left(source, h):
        return line_copy(source, h, me - 2, send_line.at[source, h])

    def to_right(source, h):
        return line_copy(source, h, me + 2, send_line.at[source, h])

    def own_right(h):
        return line_copy(chip, h, me + 2, send_right.at[h])

    pl.semaphore_wait(barrier, 1 + has_left.astype(jnp.int32) + has_right.astype(jnp.int32))
    for h in range(kvh):
        piece = kv.at[chip, h, :, core]
        pltpu.make_async_copy(piece, piece, load_sem.at[h]).wait()
        pl.when(has_left)(lambda: to_left(chip, h).start())
        pl.when(has_right)(lambda: own_right(h).start())
        pair_copy(chip, h).start()

    for h in range(kvh):
        cols = pl.ds(h * DH, DH)
        pltpu.make_async_copy(nk_hbm.at[:, cols], own.at[h, 0], own_sem.at[h]).start()
        pltpu.make_async_copy(nv_hbm.at[:, cols], own.at[h, 1], own_sem.at[h]).start()
        for g in range(group):
            pltpu.make_async_copy(
                q_hbm.at[:, pl.ds((h * group + g) * DH, DH)], qs.at[h, pl.ds(g * BS, BS)], q_sem.at[h]
            ).start()

    length = length_ref[0]
    for b in range(2 * chips):
        hits = [(table_ref[0, j] == b) & (j < length) for j in range(entries)]
        penalty[b] = jnp.where(functools.reduce(jnp.logical_or, hits), 0.0, HIDDEN)

    def scores_of(query, keys):
        return lax.dot_general(query, keys, (((1,), (1,)), ((), ())), preferred_element_type=jnp.float32)

    def own_tokens(h, _):
        pltpu.make_async_copy(qs.at[h], qs.at[h], q_sem.at[h]).wait()
        pltpu.make_async_copy(own.at[h], own.at[h], own_sem.at[h]).wait()
        token = lax.broadcasted_iota(jnp.int32, (rows, BS), 0) % BS
        causal = lax.broadcasted_iota(jnp.int32, (rows, BS), 1) <= token
        scores = jnp.where(causal, scores_of(qs[h], own[h, 0]), -HIDDEN)
        best = jnp.broadcast_to(jnp.max(scores, axis=-1, keepdims=True), (rows, DH))
        weights = jnp.exp2((scores - best) * factor)
        summed = jnp.dot(weights.astype(jnp.bfloat16), own[h, 1], preferred_element_type=jnp.float32)
        top[h] = best
        total[h] = weights
        acc[h] = summed
        return 0

    def absorb(source, h):
        keys = kv[source, h, 0].reshape(2 * BS, DH)
        values = kv[source, h, 1].reshape(2 * BS, DH)
        low, high = penalty[2 * source], penalty[2 * source + 1]
        old, old_total, old_acc = top[h], total[h], acc[h]
        scores = scores_of(qs[h], keys)
        first, second = scores[:, :BS] - low, scores[:, BS:] - high
        best = jnp.max(jnp.maximum(first, second), axis=-1, keepdims=True)
        best = jnp.maximum(old, jnp.broadcast_to(best, (rows, DH)))
        shrink = jnp.exp2((old - best) * factor)
        first = jnp.exp2((first - best) * factor)
        second = jnp.exp2((second - best) * factor)
        weights = jnp.concatenate([first.astype(jnp.bfloat16), second.astype(jnp.bfloat16)], axis=1)
        summed = jnp.dot(weights, values, preferred_element_type=jnp.float32)
        top[h] = best
        total[h] = shrink * old_total + (first + second)
        acc[h] = shrink * old_acc + summed

    def finish(h):
        whole = jnp.sum(total[h], axis=-1, keepdims=True)
        result = (acc[h] * (1.0 / whole)).astype(jnp.bfloat16)
        for g in range(group):
            cols = pl.ds(pl.multiple_of((h * group + g) * DH, DH), DH)
            out[:, cols] = result[g * BS:(g + 1) * BS]

    def own_chip(h, _):
        pair_copy(chip, h).wait_recv()
        absorb(chip, h)
        pl.when(inner)(lambda: forward(h))
        return 0

    def forward(i):
        far, h = 1 + i // kvh, i % kvh
        before, after = chip - far, chip + far

        @pl.when(after < chips)
        def _():
            line_copy(after, h, partner, send_line.at[after, h]).wait_recv()
            pl.when(has_left)(lambda: to_left(after, h).start())
            pair_copy(after, h).start()

        @pl.when(before >= 0)
        def _():
            line_copy(before, h, partner, send_line.at[before, h]).wait_recv()
            pl.when(has_right)(lambda: to_right(before, h).start())
            pair_copy(before, h).start()

    def sent(far, h):
        before, after = chip - far, chip + far

        @pl.when(after < chips)
        def _():
            pl.when(has_left)(lambda: to_left(after, h).wait_send())
            pair_copy(after, h).wait_send()

        @pl.when(before >= 0)
        def _():
            pl.when(has_right)(lambda: to_right(before, h).wait_send())
            pair_copy(before, h).wait_send()

    def own_sent(h):
        pl.when(has_left)(lambda: to_left(chip, h).wait_send())
        pl.when(has_right)(lambda: own_right(h).wait_send())
        pair_copy(chip, h).wait_send()

    def step(i, _):
        far, h = 1 + i // kvh, i % kvh
        before, after = chip - far, chip + far
        pl.when(jnp.logical_not(inner) & (i + 1 < items))(lambda: forward(i + 1))
        pl.when(far == 1)(lambda: own_sent(h))
        pl.when(far > 1)(lambda: sent(far - 1, h))

        @pl.when(after < chips)
        def _():
            pair_copy(after, h).wait_recv()
            absorb(after, h)

        @pl.when(before >= 0)
        def _():
            pair_copy(before, h).wait_recv()
            absorb(before, h)

        pl.when(inner & (i + kvh < items))(lambda: forward(i + kvh))
        pl.when(far == chips - 1)(lambda: finish(h))
        return 0

    lax.fori_loop(0, kvh, own_tokens, 0)
    lax.fori_loop(0, kvh, own_chip, 0)
    pl.when(jnp.logical_not(inner))(lambda: forward(0))
    lax.fori_loop(0, items, step, 0)
    for h in range(kvh):
        sent(chips - 1, h)


def body(chips, queries, new_keys, new_values, prefix_keys, prefix_values, block_table, prefix_blocks):
    tokens, width = queries.shape
    kvh = new_keys.shape[1] // DH
    group = width // DH // kvh
    rows = group * tokens
    entries = block_table.shape[1]
    smem = pl.BlockSpec(memory_space=pltpu.SMEM)
    anywhere = pl.BlockSpec(memory_space=pl.ANY)
    dma = pltpu.SemaphoreType.DMA
    keys = (2 * chips + 1) * BS
    return pl.pallas_call(
        functools.partial(kernel, chips, kvh, group, entries),
        out_shape=pltpu.VMEM((tokens, width), jnp.bfloat16),
        in_specs=[smem, smem] + [anywhere] * 5,
        out_specs=pl.BlockSpec(memory_space=pltpu.VMEM),
        scratch_shapes=[
            pltpu.VMEM((kvh, rows, DH), jnp.bfloat16),
            pltpu.VMEM((kvh, 2, tokens, DH), jnp.bfloat16),
            pltpu.VMEM((chips, kvh, 2, 2, BS, DH), jnp.bfloat16),
            pltpu.VMEM((kvh, rows, DH), jnp.float32),
            pltpu.VMEM((kvh, rows, DH), jnp.float32),
            pltpu.VMEM((kvh, rows, DH), jnp.float32),
            pltpu.SMEM((2 * chips,), jnp.float32),
            dma((kvh,)),
            dma((kvh,)),
            dma((kvh,)),
            dma((chips, kvh)),
            dma((chips, kvh)),
            dma((chips, kvh)),
            dma((kvh,)),
            dma((chips, kvh)),
        ],
        compiler_params=pltpu.CompilerParams(
            collective_id=0, has_side_effects=True, vmem_limit_bytes=57 * 1024 * 1024
        ),
        cost_estimate=pl.CostEstimate(
            flops=4 * kvh * rows * keys * DH, bytes_accessed=4 * tokens * width, transcendentals=kvh * rows * keys
        ),
    )(block_table, prefix_blocks, queries, new_keys, new_values, prefix_keys, prefix_values)


def solution(mesh):
    rows = P(("grp", "blk"), None)
    return jax.shard_map(
        functools.partial(body, mesh.shape["blk"] // 2),
        mesh=mesh,
        in_specs=(rows,) * 6 + (P(("grp", "blk")),),
        out_specs=rows,
        check_vma=False,
    )
```

```python
import functools

import jax
import jax.numpy as jnp
from jax import lax
from jax.experimental import pallas as pl
from jax.experimental.pallas import tpu as pltpu
from jax.sharding import PartitionSpec as P

DH = 128
BS = 128
MESH = pl.DeviceIdType.MESH
LOG2E = 1.4426950408889634
HIDDEN = 1e38


def kernel(
    chips, kvh, group, entries,
    table_ref, length_ref, q_hbm, nk_hbm, nv_hbm, pk_hbm, pv_hbm, out,
    qs, own, kv, acc, top, total, penalty,
    q_sem, own_sem, load_sem, recv_line, recv_pair, send_line, send_right, send_pair,
):
    me = lax.axis_index("blk")
    chip = me // 2
    core = me - 2 * chip
    partner = 2 * chip + 1 - core
    rows = group * BS
    factor = LOG2E * DH ** -0.5
    has_left, has_right = chip > 0, chip < chips - 1
    inner = has_left & has_right
    items = kvh * (chips - 1)

    barrier = pltpu.get_barrier_semaphore()

    def greet(device):
        pl.semaphore_signal(barrier, inc=1, device_id={"blk": device}, device_id_type=MESH)

    greet(partner)
    pl.when(has_left)(lambda: greet(me - 2))
    pl.when(has_right)(lambda: greet(me + 2))

    for h in range(kvh):
        cols = pl.ds(h * DH, DH)
        pltpu.make_async_copy(pk_hbm.at[:, cols], kv.at[chip, h, 0, core], load_sem.at[h]).start()
        pltpu.make_async_copy(pv_hbm.at[:, cols], kv.at[chip, h, 1, core], load_sem.at[h]).start()
    def line_copy(source, h, device, sem):
        piece = kv.at[source, h, :, core]
        return pltpu.make_async_remote_copy(
            src_ref=piece, dst_ref=piece, send_sem=sem, recv_sem=recv_line.at[source, h],
            device_id={"blk": device}, device_id_type=MESH,
        )

    def pair_copy(source, h):
        piece = kv.at[source, h, :, core]
        return pltpu.make_async_remote_copy(
            src_ref=piece, dst_ref=piece, send_sem=send_pair.at[source, h], recv_sem=recv_pair.at[source, h],
            device_id={"blk": partner}, device_id_type=MESH,
        )

    def to_left(source, h):
        return line_copy(source, h, me - 2, send_line.at[source, h])

    def to_right(source, h):
        return line_copy(source, h, me + 2, send_line.at[source, h])

    def own_right(h):
        return line_copy(chip, h, me + 2, send_right.at[h])

    pl.semaphore_wait(barrier, 1 + has_left.astype(jnp.int32) + has_right.astype(jnp.int32))
    for h in range(kvh):
        piece = kv.at[chip, h, :, core]
        pltpu.make_async_copy(piece, piece, load_sem.at[h]).wait()
        pl.when(has_left)(lambda: to_left(chip, h).start())
        pl.when(has_right)(lambda: own_right(h).start())
        pair_copy(chip, h).start()

    for h in range(kvh):
        cols = pl.ds(h * DH, DH)
        pltpu.make_async_copy(nk_hbm.at[:, cols], own.at[h, 0], own_sem.at[h]).start()
        pltpu.make_async_copy(nv_hbm.at[:, cols], own.at[h, 1], own_sem.at[h]).start()
        for g in range(group):
            pltpu.make_async_copy(
                q_hbm.at[:, pl.ds((h * group + g) * DH, DH)], qs.at[h, pl.ds(g * BS, BS)], q_sem.at[h]
            ).start()

    length = length_ref[0]
    for b in range(2 * chips):
        hits = [(table_ref[0, j] == b) & (j < length) for j in range(entries)]
        penalty[b] = jnp.where(functools.reduce(jnp.logical_or, hits), 0.0, HIDDEN)

    def scores_of(query, keys):
        return lax.dot_general(query, keys, (((1,), (1,)), ((), ())), preferred_element_type=jnp.float32)

    def own_tokens(h, _):
        pltpu.make_async_copy(qs.at[h], qs.at[h], q_sem.at[h]).wait()
        pltpu.make_async_copy(own.at[h], own.at[h], own_sem.at[h]).wait()
        token = lax.broadcasted_iota(jnp.int32, (rows, BS), 0) % BS
        causal = lax.broadcasted_iota(jnp.int32, (rows, BS), 1) <= token
        scores = jnp.where(causal, scores_of(qs[h], own[h, 0]), -HIDDEN)
        best = jnp.broadcast_to(jnp.max(scores, axis=-1, keepdims=True), (rows, DH))
        weights = jnp.exp2((scores - best) * factor)
        summed = jnp.dot(weights.astype(jnp.bfloat16), own[h, 1], preferred_element_type=jnp.float32)
        top[h] = best
        total[h] = weights
        acc[h] = summed
        return 0

    def absorb(source, h):
        keys = kv[source, h, 0].reshape(2 * BS, DH)
        values = kv[source, h, 1].reshape(2 * BS, DH)
        low, high = penalty[2 * source], penalty[2 * source + 1]
        old, old_total, old_acc = top[h], total[h], acc[h]
        scores = scores_of(qs[h], keys)
        first, second = scores[:, :BS] - low, scores[:, BS:] - high
        best = jnp.max(jnp.maximum(first, second), axis=-1, keepdims=True)
        best = jnp.maximum(old, jnp.broadcast_to(best, (rows, DH)))
        shrink = jnp.exp2((old - best) * factor)
        first = jnp.exp2((first - best) * factor)
        second = jnp.exp2((second - best) * factor)
        weights = jnp.concatenate([first.astype(jnp.bfloat16), second.astype(jnp.bfloat16)], axis=1)
        summed = jnp.dot(weights, values, preferred_element_type=jnp.float32)
        top[h] = best
        total[h] = shrink * old_total + (first + second)
        acc[h] = shrink * old_acc + summed

    def absorb_one(source, h, side):
        old, old_total, old_acc = top[h], total[h], acc[h]
        scores = scores_of(qs[h], kv[source, h, 0, side]) - penalty[2 * source + side]
        best = jnp.maximum(old, jnp.broadcast_to(jnp.max(scores, axis=-1, keepdims=True), (rows, DH)))
        shrink = jnp.exp2((old - best) * factor)
        weights = jnp.exp2((scores - best) * factor)
        summed = jnp.dot(weights.astype(jnp.bfloat16), kv[source, h, 1, side], preferred_element_type=jnp.float32)
        top[h] = best
        total[h] = shrink * old_total + weights
        acc[h] = shrink * old_acc + summed

    def finish(h):
        whole = jnp.sum(total[h], axis=-1, keepdims=True)
        result = (acc[h] * (1.0 / whole)).astype(jnp.bfloat16)
        for g in range(group):
            cols = pl.ds(pl.multiple_of((h * group + g) * DH, DH), DH)
            out[:, cols] = result[g * BS:(g + 1) * BS]

    def own_chip(h, _):
        pair_copy(chip, h).wait_recv()
        absorb(chip, h)
        pl.when(inner)(lambda: forward(h))
        return 0

    def forward(i):
        far, h = 1 + i // kvh, i % kvh
        before, after = chip - far, chip + far

        @pl.when(after < chips)
        def _():
            line_copy(after, h, partner, send_line.at[after, h]).wait_recv()
            pl.when(has_left)(lambda: to_left(after, h).start())
            pair_copy(after, h).start()

        @pl.when(before >= 0)
        def _():
            line_copy(before, h, partner, send_line.at[before, h]).wait_recv()
            pl.when(has_right)(lambda: to_right(before, h).start())
            pair_copy(before, h).start()

    def sent(far, h):
        before, after = chip - far, chip + far

        @pl.when(after < chips)
        def _():
            pl.when(has_left)(lambda: to_left(after, h).wait_send())
            pair_copy(after, h).wait_send()

        @pl.when(before >= 0)
        def _():
            pl.when(has_right)(lambda: to_right(before, h).wait_send())
            pair_copy(before, h).wait_send()

    def own_sent(h):
        pl.when(has_left)(lambda: to_left(chip, h).wait_send())
        pl.when(has_right)(lambda: own_right(h).wait_send())
        pair_copy(chip, h).wait_send()

    def step(i, _):
        far, h = 1 + i // kvh, i % kvh
        before, after = chip - far, chip + far
        pl.when(jnp.logical_not(inner) & has_right)(lambda: absorb_one(after, h, core))
        pl.when(jnp.logical_not(inner) & has_left)(lambda: absorb_one(before, h, core))
        pl.when(jnp.logical_not(inner) & (i + 1 < items))(lambda: forward(i + 1))
        pl.when(far == 1)(lambda: own_sent(h))
        pl.when(far > 1)(lambda: sent(far - 1, h))

        @pl.when(after < chips)
        def _():
            pair_copy(after, h).wait_recv()
            pl.when(inner)(lambda: absorb(after, h))
            pl.when(jnp.logical_not(inner))(lambda: absorb_one(after, h, 1 - core))

        @pl.when(before >= 0)
        def _():
            pair_copy(before, h).wait_recv()
            pl.when(inner)(lambda: absorb(before, h))
            pl.when(jnp.logical_not(inner))(lambda: absorb_one(before, h, 1 - core))

        pl.when(inner & (i + kvh < items))(lambda: forward(i + kvh))
        pl.when(far == chips - 1)(lambda: finish(h))
        return 0

    lax.fori_loop(0, kvh, own_tokens, 0)
    lax.fori_loop(0, kvh, own_chip, 0)
    pl.when(jnp.logical_not(inner))(lambda: forward(0))
    lax.fori_loop(0, items, step, 0)
    for h in range(kvh):
        sent(chips - 1, h)


def body(chips, queries, new_keys, new_values, prefix_keys, prefix_values, block_table, prefix_blocks):
    tokens, width = queries.shape
    kvh = new_keys.shape[1] // DH
    group = width // DH // kvh
    rows = group * tokens
    entries = block_table.shape[1]
    smem = pl.BlockSpec(memory_space=pltpu.SMEM)
    anywhere = pl.BlockSpec(memory_space=pl.ANY)
    dma = pltpu.SemaphoreType.DMA
    keys = (2 * chips + 1) * BS
    return pl.pallas_call(
        functools.partial(kernel, chips, kvh, group, entries),
        out_shape=pltpu.VMEM((tokens, width), jnp.bfloat16),
        in_specs=[smem, smem] + [anywhere] * 5,
        out_specs=pl.BlockSpec(memory_space=pltpu.VMEM),
        scratch_shapes=[
            pltpu.VMEM((kvh, rows, DH), jnp.bfloat16),
            pltpu.VMEM((kvh, 2, tokens, DH), jnp.bfloat16),
            pltpu.VMEM((chips, kvh, 2, 2, BS, DH), jnp.bfloat16),
            pltpu.VMEM((kvh, rows, DH), jnp.float32),
            pltpu.VMEM((kvh, rows, DH), jnp.float32),
            pltpu.VMEM((kvh, rows, DH), jnp.float32),
            pltpu.SMEM((2 * chips,), jnp.float32),
            dma((kvh,)),
            dma((kvh,)),
            dma((kvh,)),
            dma((chips, kvh)),
            dma((chips, kvh)),
            dma((chips, kvh)),
            dma((kvh,)),
            dma((chips, kvh)),
        ],
        compiler_params=pltpu.CompilerParams(
            collective_id=0, has_side_effects=True, vmem_limit_bytes=57 * 1024 * 1024
        ),
        cost_estimate=pl.CostEstimate(
            flops=4 * kvh * rows * keys * DH, bytes_accessed=4 * tokens * width, transcendentals=kvh * rows * keys
        ),
    )(block_table, prefix_blocks, queries, new_keys, new_values, prefix_keys, prefix_values)


def solution(mesh):
    rows = P(("grp", "blk"), None)
    return jax.shard_map(
        functools.partial(body, mesh.shape["blk"] // 2),
        mesh=mesh,
        in_specs=(rows,) * 6 + (P(("grp", "blk")),),
        out_specs=rows,
        check_vma=False,
    )
```

```python
import functools

import jax
import jax.numpy as jnp
from jax import lax
from jax.experimental import pallas as pl
from jax.experimental.pallas import tpu as pltpu
from jax.sharding import PartitionSpec as P

DH = 128
BS = 128
MESH = pl.DeviceIdType.MESH
LOG2E = 1.4426950408889634
HIDDEN = 1e38


def kernel(
    chips, kvh, group, entries,
    table_ref, length_ref, q_hbm, nk_hbm, nv_hbm, pk_hbm, pv_hbm, out,
    qs, own, kv, acc, top, total, penalty,
    q_sem, own_sem, load_sem, recv_line, recv_pair, send_line, send_right, send_pair,
):
    me = lax.axis_index("blk")
    chip = me // 2
    core = me - 2 * chip
    partner = 2 * chip + 1 - core
    rows = group * BS
    factor = LOG2E * DH ** -0.5
    has_left, has_right = chip > 0, chip < chips - 1
    inner = has_left & has_right
    items = kvh * (chips - 1)

    barrier = pltpu.get_barrier_semaphore()

    def greet(device):
        pl.semaphore_signal(barrier, inc=1, device_id={"blk": device}, device_id_type=MESH)

    greet(partner)
    pl.when(has_left)(lambda: greet(me - 2))
    pl.when(has_right)(lambda: greet(me + 2))

    for h in range(kvh):
        cols = pl.ds(h * DH, DH)
        pltpu.make_async_copy(pk_hbm.at[:, cols], kv.at[chip, h, 0, core], load_sem.at[h]).start()
        pltpu.make_async_copy(pv_hbm.at[:, cols], kv.at[chip, h, 1, core], load_sem.at[h]).start()
    def line_copy(source, h, device, sem):
        piece = kv.at[source, h, :, core]
        return pltpu.make_async_remote_copy(
            src_ref=piece, dst_ref=piece, send_sem=sem, recv_sem=recv_line.at[source, h],
            device_id={"blk": device}, device_id_type=MESH,
        )

    def pair_copy(source, h):
        piece = kv.at[source, h, :, core]
        return pltpu.make_async_remote_copy(
            src_ref=piece, dst_ref=piece, send_sem=send_pair.at[source, h], recv_sem=recv_pair.at[source, h],
            device_id={"blk": partner}, device_id_type=MESH,
        )

    def to_left(source, h):
        return line_copy(source, h, me - 2, send_line.at[source, h])

    def to_right(source, h):
        return line_copy(source, h, me + 2, send_line.at[source, h])

    def own_right(h):
        return line_copy(chip, h, me + 2, send_right.at[h])

    pl.semaphore_wait(barrier, 1 + has_left.astype(jnp.int32) + has_right.astype(jnp.int32))
    for h in range(kvh):
        piece = kv.at[chip, h, :, core]
        pltpu.make_async_copy(piece, piece, load_sem.at[h]).wait()
        pl.when(has_left)(lambda: to_left(chip, h).start())
        pl.when(has_right)(lambda: own_right(h).start())
    for h in range(kvh):
        pair_copy(chip, h).start()

    for h in range(kvh):
        cols = pl.ds(h * DH, DH)
        pltpu.make_async_copy(nk_hbm.at[:, cols], own.at[h, 0], own_sem.at[h]).start()
        pltpu.make_async_copy(nv_hbm.at[:, cols], own.at[h, 1], own_sem.at[h]).start()
        for g in range(group):
            pltpu.make_async_copy(
                q_hbm.at[:, pl.ds((h * group + g) * DH, DH)], qs.at[h, pl.ds(g * BS, BS)], q_sem.at[h]
            ).start()

    length = length_ref[0]
    for b in range(2 * chips):
        hits = [(table_ref[0, j] == b) & (j < length) for j in range(entries)]
        penalty[b] = jnp.where(functools.reduce(jnp.logical_or, hits), 0.0, HIDDEN)

    def scores_of(query, keys):
        return lax.dot_general(query, keys, (((1,), (1,)), ((), ())), preferred_element_type=jnp.float32)

    def own_tokens(h, _):
        pltpu.make_async_copy(qs.at[h], qs.at[h], q_sem.at[h]).wait()
        pltpu.make_async_copy(own.at[h], own.at[h], own_sem.at[h]).wait()
        token = lax.broadcasted_iota(jnp.int32, (rows, BS), 0) % BS
        causal = lax.broadcasted_iota(jnp.int32, (rows, BS), 1) <= token
        scores = jnp.where(causal, scores_of(qs[h], own[h, 0]), -HIDDEN)
        best = jnp.broadcast_to(jnp.max(scores, axis=-1, keepdims=True), (rows, DH))
        weights = jnp.exp2((scores - best) * factor)
        summed = jnp.dot(weights.astype(jnp.bfloat16), own[h, 1], preferred_element_type=jnp.float32)
        top[h] = best
        total[h] = weights
        acc[h] = summed
        return 0

    def absorb(source, h):
        keys = kv[source, h, 0].reshape(2 * BS, DH)
        values = kv[source, h, 1].reshape(2 * BS, DH)
        low, high = penalty[2 * source], penalty[2 * source + 1]
        old, old_total, old_acc = top[h], total[h], acc[h]
        scores = scores_of(qs[h], keys)
        first, second = scores[:, :BS] - low, scores[:, BS:] - high
        best = jnp.max(jnp.maximum(first, second), axis=-1, keepdims=True)
        best = jnp.maximum(old, jnp.broadcast_to(best, (rows, DH)))
        shrink = jnp.exp2((old - best) * factor)
        first = jnp.exp2((first - best) * factor)
        second = jnp.exp2((second - best) * factor)
        weights = jnp.concatenate([first.astype(jnp.bfloat16), second.astype(jnp.bfloat16)], axis=1)
        summed = jnp.dot(weights, values, preferred_element_type=jnp.float32)
        top[h] = best
        total[h] = shrink * old_total + (first + second)
        acc[h] = shrink * old_acc + summed

    def finish(h):
        whole = jnp.sum(total[h], axis=-1, keepdims=True)
        result = (acc[h] * (1.0 / whole)).astype(jnp.bfloat16)
        for g in range(group):
            cols = pl.ds(pl.multiple_of((h * group + g) * DH, DH), DH)
            out[:, cols] = result[g * BS:(g + 1) * BS]

    def own_chip(h, _):
        pair_copy(chip, h).wait_recv()
        absorb(chip, h)
        pl.when(inner)(lambda: forward(h))
        return 0

    def forward(i):
        far, h = 1 + i // kvh, i % kvh
        before, after = chip - far, chip + far

        @pl.when(after < chips)
        def _():
            line_copy(after, h, partner, send_line.at[after, h]).wait_recv()
            pl.when(has_left)(lambda: to_left(after, h).start())
            pair_copy(after, h).start()

        @pl.when(before >= 0)
        def _():
            line_copy(before, h, partner, send_line.at[before, h]).wait_recv()
            pl.when(has_right)(lambda: to_right(before, h).start())
            pair_copy(before, h).start()

    def sent(far, h):
        before, after = chip - far, chip + far

        @pl.when(after < chips)
        def _():
            pl.when(has_left)(lambda: to_left(after, h).wait_send())
            pair_copy(after, h).wait_send()

        @pl.when(before >= 0)
        def _():
            pl.when(has_right)(lambda: to_right(before, h).wait_send())
            pair_copy(before, h).wait_send()

    def own_sent(h):
        pl.when(has_left)(lambda: to_left(chip, h).wait_send())
        pl.when(has_right)(lambda: own_right(h).wait_send())
        pair_copy(chip, h).wait_send()

    def step(i, _):
        far, h = 1 + i // kvh, i % kvh
        before, after = chip - far, chip + far
        pl.when(jnp.logical_not(inner) & (i + 1 < items))(lambda: forward(i + 1))
        pl.when(far == 1)(lambda: own_sent(h))
        pl.when(far > 1)(lambda: sent(far - 1, h))

        @pl.when(after < chips)
        def _():
            pair_copy(after, h).wait_recv()
            absorb(after, h)

        @pl.when(before >= 0)
        def _():
            pair_copy(before, h).wait_recv()
            absorb(before, h)

        pl.when(inner & (i + kvh < items))(lambda: forward(i + kvh))
        pl.when(far == chips - 1)(lambda: finish(h))
        return 0

    lax.fori_loop(0, kvh, own_tokens, 0)
    lax.fori_loop(0, kvh, own_chip, 0)
    pl.when(jnp.logical_not(inner))(lambda: forward(0))
    lax.fori_loop(0, items, step, 0)
    for h in range(kvh):
        sent(chips - 1, h)


def body(chips, queries, new_keys, new_values, prefix_keys, prefix_values, block_table, prefix_blocks):
    tokens, width = queries.shape
    kvh = new_keys.shape[1] // DH
    group = width // DH // kvh
    rows = group * tokens
    entries = block_table.shape[1]
    smem = pl.BlockSpec(memory_space=pltpu.SMEM)
    anywhere = pl.BlockSpec(memory_space=pl.ANY)
    dma = pltpu.SemaphoreType.DMA
    keys = (2 * chips + 1) * BS
    return pl.pallas_call(
        functools.partial(kernel, chips, kvh, group, entries),
        out_shape=pltpu.VMEM((tokens, width), jnp.bfloat16),
        in_specs=[smem, smem] + [anywhere] * 5,
        out_specs=pl.BlockSpec(memory_space=pltpu.VMEM),
        scratch_shapes=[
            pltpu.VMEM((kvh, rows, DH), jnp.bfloat16),
            pltpu.VMEM((kvh, 2, tokens, DH), jnp.bfloat16),
            pltpu.VMEM((chips, kvh, 2, 2, BS, DH), jnp.bfloat16),
            pltpu.VMEM((kvh, rows, DH), jnp.float32),
            pltpu.VMEM((kvh, rows, DH), jnp.float32),
            pltpu.VMEM((kvh, rows, DH), jnp.float32),
            pltpu.SMEM((2 * chips,), jnp.float32),
            dma((kvh,)),
            dma((kvh,)),
            dma((kvh,)),
            dma((chips, kvh)),
            dma((chips, kvh)),
            dma((chips, kvh)),
            dma((kvh,)),
            dma((chips, kvh)),
        ],
        compiler_params=pltpu.CompilerParams(
            collective_id=0, has_side_effects=True, vmem_limit_bytes=57 * 1024 * 1024
        ),
        cost_estimate=pl.CostEstimate(
            flops=4 * kvh * rows * keys * DH, bytes_accessed=4 * tokens * width, transcendentals=kvh * rows * keys
        ),
    )(block_table, prefix_blocks, queries, new_keys, new_values, prefix_keys, prefix_values)


def solution(mesh):
    rows = P(("grp", "blk"), None)
    return jax.shard_map(
        functools.partial(body, mesh.shape["blk"] // 2),
        mesh=mesh,
        in_specs=(rows,) * 6 + (P(("grp", "blk")),),
        out_specs=rows,
        check_vma=False,
    )
```
